32 devices in a mesh: chan: 8 (over z, y), tm: 4 (over x, core).
Axes of the slice: x: 2, y: 2, z: 4, core: 2. Of those that a mesh axis runs over, the one named last changes fastest.
Arguments:
- traces: float32 [640, 8192], P('chan', 'tm'), may hold values from -6 to 6
- fir_taps: float32 [65], replicated, may hold values from -0.75 to 0.75
- source_index: int32 [64], replicated, may hold values from 0 to 639, as said below
Outputs:
- correlation: float32 [4, 64, 640, 512], P('tm', None, 'chan')
The draws below stay inside these ranges and needn't reach their ends.
Inputs may be any that keep to these rules, and one draw needn't show every extreme that they name: `source_index`: the 64 channel numbers are distinct. They lie in 8 consecutive blocks of 80 channels (block b holding channels b * 80 to b * 80 + 79, counted around the fibre's end), at most 12 in one block, and exactly 12 in some block. Channels 0 and 639 are always among them.
All inputs are finite; a program needn't handle non-finite values.
Results may differ from the reference program's by a relative error of at most 0.0029.
Values may be sent and summed in bfloat16 or wider, within the bound.
No kernel may reach another device: no remote copies, remote signals or barrier semaphores. Data moves between devices by JAX's collectives and lax.ppermute only.
A program may use at most 192 MiB of HBM per device.

```python
import math
import jax
import jax.numpy as jnp
import numpy as np
from jax import lax

CH = 80
T_DEV = 2048
LAG_HALF = 256
FIR_HALF = 32
NORM_HALF = 64
FIR_TAPS = 65
NCH = 640
NT = 8192
N_TM = 4


def draw_source_index(key, part):
    block_total = NCH // CH
    counts = np.array([12, 12, 10, 8, 8, 6, 4, 4])
    starts = jnp.array(np.concatenate([[0], np.cumsum(counts)[:-1]]), jnp.int32)
    start_key, perm_key, order_key = jax.random.split(key, 3)
    first = jax.random.randint(start_key, (), block_total - 7, block_total)
    block_of = (first + jnp.arange(8)) % block_total
    within = jax.vmap(lambda k: jax.random.permutation(k, CH))(jax.random.split(perm_key, 8))
    target = jnp.where(block_of == 0, 0, CH - 1).astype(jnp.int32)
    forced = (block_of == 0) | (block_of == block_total - 1)
    column = jnp.arange(CH)[None, :]
    leading = within[:, :1]
    swapped = jnp.where(within == target[:, None], leading, jnp.where(column == 0, target[:, None], within))
    within = jnp.where(forced[:, None], swapped, within)
    number = jnp.arange(64)
    rank_of = jnp.sum((number[:, None] >= starts[None, 1:]).astype(jnp.int32), axis=1)
    place = number - starts[rank_of]
    channel = block_of[rank_of] * CH + within[rank_of, place]
    order = jax.random.permutation(order_key, 64)
    return channel[order].astype(jnp.int32)


def block_scale(own_key, dims, shards, least, largest):
    loudness, own = 1.0, jax.random.fold_in(own_key, 6)
    for position, shards_of in shards:
        heights = jnp.exp(jax.random.uniform(jax.random.fold_in(own, position), (shards_of,), jnp.float32, least / len(shards), largest / len(shards)))
        loudness = loudness * jnp.repeat(heights, dims[position] // shards_of).reshape([-1 if axis == position else 1 for axis in range(len(dims))])
    return loudness


def normal_values(own_key, extent, width, limit, cuts=(), kind=jnp.bfloat16):
    entries = jax.random.normal(own_key, extent, jnp.float32) * width
    if len(cuts) > 0:
        entries = block_scale(own_key, extent, cuts, -0.22, 0.18) * entries
    return jnp.clip(entries, min=-limit, max=limit).astype(kind)


def setup_inputs(seed: int = 0) -> dict:
    keys = jax.random.split(jax.random.key(seed), 4)
    return {
        "traces": normal_values(keys[0], (NCH, NT), 1.0, 6.0, ((0, 8), (1, 4)), jnp.float32),
        "fir_taps": normal_values(keys[1], (FIR_TAPS,), FIR_TAPS ** -0.5, 0.75, (), jnp.float32),
        "source_index": draw_source_index(jax.random.fold_in(keys[3], 71), 0),
    }


EPSILON = 1e-05

def bandpass(padded, fir_taps):
    result = lax.conv_general_dilated(padded[:, None, :], fir_taps[None, None, :], (1,), 'VALID', dimension_numbers=('NCH', 'OIH', 'NCH'), precision=lax.Precision.HIGHEST)
    return result[:, 0, :]

def reference(traces, fir_taps, source_index):
    padded = jnp.pad(traces, ((0, 0), (FIR_HALF, FIR_HALF)))
    filtered = bandpass(padded, fir_taps)
    filtered_wide = jnp.pad(filtered, ((0, 0), (NORM_HALF, NORM_HALF)))
    window_sum = lax.reduce_window(jnp.abs(filtered_wide), jnp.zeros((), filtered_wide.dtype), lax.add, (1, 2 * NORM_HALF + 1), (1, 1), 'VALID')
    normed = (filtered / (EPSILON + window_sum / (2 * NORM_HALF + 1))).astype(jnp.bfloat16)
    sources = jnp.take(normed, source_index, axis=0).astype(jnp.float32)
    source_pad = jnp.pad(sources, ((0, 0), (LAG_HALF, LAG_HALF)))
    lag_width = min(128, 2 * LAG_HALF)
    slab_results = []
    for g in range(N_TM):
        window = source_pad[:, g * T_DEV:g * T_DEV + T_DEV + 2 * LAG_HALF]
        receivers = normed[:, g * T_DEV:(g + 1) * T_DEV].astype(jnp.float32)
        pieces = []
        for i in range(2 * LAG_HALF // lag_width):
            hankel = jnp.stack([window[:, i * lag_width + j:i * lag_width + j + T_DEV] for j in range(lag_width)], axis=1)
            pieces.append(jnp.einsum('sjt,ct->scj', hankel, receivers, precision=lax.Precision.HIGHEST))
        slab_results.append(jnp.concatenate(pieces, axis=2) / math.sqrt(T_DEV))
    return jnp.stack(slab_results, axis=0)
```

```python
import functools
import math

import jax
import jax.numpy as jnp
from jax import lax
from jax.experimental import pallas as pl
from jax.experimental.pallas import tpu as pltpu
from jax.sharding import PartitionSpec as P

LAG_HALF = 256
NORM_HALF = 64
MAX_OWN = 12
EPSILON = 1e-05

LANES = 128
LAG_WIDTH = 32
PIECES = LANES // LAG_WIDTH
LAG_BLOCKS = 2 * LAG_HALF // LANES
SIDE = 3
EDGE = LAG_HALF // LANES
GROUP = 8
MIB = 2**20
F32 = jnp.float32
BF16 = jnp.bfloat16


def split(value):
    high = value.astype(BF16)
    return high, (value - high.astype(F32)).astype(BF16)


def dot_t(left, right):
    return lax.dot_general(left, right, (((1,), (1,)), ((), ())), preferred_element_type=F32)


def stacked(blocks):
    wide = [
        jnp.concatenate([blocks[b - 1], blocks[b], blocks[b + 1]], axis=1)
        for b in range(1, len(blocks) - 1)
    ]
    return jnp.concatenate(wide, axis=0)


def normalize(blocks, first, last, has_low, has_high, taps_row, fir_taps):
    rows = blocks[0].shape[0]
    row = lax.broadcasted_iota(jnp.int32, (LANES, 3 * LANES), 0)
    lane = lax.broadcasted_iota(jnp.int32, (LANES, 3 * LANES), 1)
    toeplitz = pltpu.roll(jnp.broadcast_to(taps_row, (LANES, 3 * LANES)), 0, 1, stride=1, stride_axis=0)
    taps_high, taps_low = split(toeplitz)
    reach = lane - row - (LANES - NORM_HALF)
    band = jnp.where((reach >= 0) & (reach <= 2 * NORM_HALF), 1.0, 0.0).astype(BF16)
    wide_high, wide_low = [], []
    pairs = [split(block) for block in blocks]
    wide_high = stacked([p[0] for p in pairs])
    wide_low = stacked([p[1] for p in pairs])
    filtered = dot_t(wide_high, taps_high) + dot_t(wide_low, taps_high) + dot_t(wide_high, taps_low)
    inner = []
    for k in range(len(blocks) - 2):
        block = filtered[k * rows : (k + 1) * rows]
        number = first + 1 + k
        if number < 0:
            block = jnp.where(has_low, block, 0.0)
        elif number > last:
            block = jnp.where(has_high, block, 0.0)
        inner.append(block)
    sizes = [split(jnp.abs(block)) for block in inner]
    total = dot_t(stacked([p[0] for p in sizes]), band) + dot_t(stacked([p[1] for p in sizes]), band)
    level = total / (2 * NORM_HALF + 1)
    return [
        block / (EPSILON + level[k * rows : (k + 1) * rows]) for k, block in enumerate(inner[1:-1])
    ]


def source_kernel(offset, place, traces, low, high, taps_row, out, rows_buf, *, fir_taps):
    samples = traces.shape[1]
    own = samples // LANES
    side = low.shape[1]
    rows_buf[...] = jnp.zeros_like(rows_buf)
    for k in range(MAX_OWN):
        at = offset[k]
        rows_buf[k : k + 1, LANES : LANES + side] = low[pl.ds(at, 1), :]
        rows_buf[k : k + 1, LANES + side : LANES + side + samples] = traces[pl.ds(at, 1), :]
        rows_buf[k : k + 1, LANES + side + samples : LANES + 2 * side + samples] = high[pl.ds(at, 1), :]
    count = rows_buf.shape[1] // LANES
    blocks = [rows_buf[:, b * LANES : (b + 1) * LANES] for b in range(count)]
    normed = normalize(
        blocks, -SIDE - 1, own - 1, place[0] > 0, place[0] < place[1] - 1, taps_row[...], fir_taps
    )
    packed = jnp.concatenate([block[:MAX_OWN] for block in normed], axis=0)
    out[...] = packed.astype(BF16)


def shifted_kernel(place, traces, low, high, taps_row, out, rows_buf, *, fir_taps):
    channels, samples = traces.shape
    own = samples // LANES
    side = low.shape[1]
    blocks = [low[:, side - 2 * LANES : side - LANES], low[:, side - LANES :]]
    blocks += [traces[:, b * LANES : (b + 1) * LANES] for b in range(own)]
    blocks += [high[:, :LANES], high[:, LANES : 2 * LANES]]
    normed = normalize(
        blocks, -2, own - 1, place[0] > 0, place[0] < place[1] - 1, taps_row[...], fir_taps
    )
    for b, block in enumerate(normed):
        rows_buf[b * channels : (b + 1) * channels, :] = block
    lane = lax.broadcasted_iota(jnp.int32, (LAG_WIDTH, LANES), 1)
    later = lane >= lax.broadcasted_iota(jnp.int32, (LAG_WIDTH, LANES), 0)

    @pl.loop(0, channels)
    def _(c):
        before = jnp.zeros((LAG_WIDTH, LANES), F32)
        at = pl.multiple_of(c * LAG_WIDTH, LAG_WIDTH)
        for b in range(own + 1):
            if b < own:
                line = rows_buf[pl.ds(b * channels + c, 1), :]
                turned = pltpu.roll(
                    jnp.broadcast_to(line, (LAG_WIDTH, LANES)), 0, 1, stride=1, stride_axis=0
                )
            else:
                turned = jnp.zeros((LAG_WIDTH, LANES), F32)
            out[pl.ds(at, LAG_WIDTH), b * LANES : (b + 1) * LANES] = jnp.where(
                later, turned, before
            ).astype(BF16)
            before = turned


def correlate_kernel(place, *refs, sources, channels, samples, pieces, scale):
    parts = refs[:pieces]
    shifted, out, all_rows, lines, windows, ready, sem = refs[pieces:]
    step = pl.program_id(0)
    slot = lax.rem(step, 2)
    depth = samples + LANES
    blocks = samples // LANES + 2 * EDGE

    def sends(at, slot):
        return [
            pltpu.make_async_copy(
                ready.at[slot, q].reshape(sources, GROUP, LANES),
                out.at[:, pl.ds(at * GROUP, GROUP), pl.ds(q * LANES, LANES)],
                sem.at[slot],
            )
            for q in range(LAG_BLOCKS)
        ]

    @pl.when(step == 0)
    def _():
        start = 0
        for part in parts:
            all_rows[start : start + part.shape[0], :] = part[...].astype(F32)
            start += part.shape[0]
        lines[blocks * sources :, :] = jnp.zeros((sources, LANES), F32)

        for s in range(sources):
            lines[pl.ds(s, blocks, stride=sources), :] = all_rows[
                pl.ds(place[s], blocks, stride=MAX_OWN), :
            ]

        lane = lax.broadcasted_iota(jnp.int32, (sources, LANES), 1)
        for p in range(PIECES):
            turn = p * LAG_WIDTH
            turned = None
            for b in range(blocks + 1):
                line = lines[b * sources : (b + 1) * sources, :]
                following = pltpu.roll(line, LANES - turn, 1) if p else line
                if b:
                    block = b - 1
                    value = jnp.where(lane < LANES - turn, turned, following).astype(BF16)
                    for q in range(LAG_BLOCKS):
                        if 0 <= block - q < depth // LANES:
                            at = (q * PIECES + p) * sources
                            windows[at : at + sources, (block - q) * LANES : (block - q + 1) * LANES] = value
                turned = following

    @pl.when(step >= 2)
    def _():
        for copy in sends(step - 2, slot):
            copy.wait()

    width = GROUP * LAG_WIDTH
    result = dot_t(windows[...], shifted[pl.ds(pl.multiple_of(step * width, width), width), :])
    lane = lax.broadcasted_iota(jnp.int32, (sources, LANES), 1)
    for q in range(LAG_BLOCKS):
        for half in range(width // LANES):
            tiles = [
                result[
                    (q * PIECES + p) * sources : (q * PIECES + p + 1) * sources,
                    half * LANES : (half + 1) * LANES,
                ]
                * scale
                for p in range(PIECES)
            ]
            gap = PIECES // 2
            while gap:
                wide = gap * LAG_WIDTH
                low_half = lax.rem(lane, 2 * wide) < wide
                for p in range(PIECES):
                    if p & gap:
                        continue
                    a, b = tiles[p], tiles[p + gap]
                    tiles[p] = jnp.where(low_half, a, pltpu.roll(b, wide, 1))
                    tiles[p + gap] = jnp.where(low_half, pltpu.roll(a, LANES - wide, 1), b)
                gap //= 2
            for p in range(PIECES):
                ready.at[slot, q][pl.ds(half * PIECES + p, sources, stride=GROUP), :] = tiles[p]
    for copy in sends(step, slot):
        copy.start()

    @pl.when(step == pl.num_programs(0) - 1)
    def _():
        for copy in sends(step - 1, 1 - slot):
            copy.wait()
        for copy in sends(step, slot):
            copy.wait()


SMEM = pl.BlockSpec(memory_space=pltpu.SMEM)
VMEM = pl.BlockSpec(memory_space=pltpu.VMEM)


def source_rows(offset, place, traces, low, high, taps_row, fir_taps):
    samples = traces.shape[1]
    blocks = samples // LANES + 2 * EDGE
    return pl.pallas_call(
        functools.partial(source_kernel, fir_taps=fir_taps),
        in_specs=[SMEM, SMEM] + [VMEM] * 4,
        out_specs=VMEM,
        out_shape=jax.ShapeDtypeStruct((blocks * MAX_OWN, LANES), BF16),
        scratch_shapes=[pltpu.VMEM((16, samples + 2 * (SIDE + 1) * LANES), F32)],
        compiler_params=pltpu.CompilerParams(vmem_limit_bytes=16 * MIB),
        name="source_rows",
    )(offset, place, traces, low, high, taps_row)


def shifted_rows(place, traces, low, high, taps_row, fir_taps):
    channels, samples = traces.shape
    return pl.pallas_call(
        functools.partial(shifted_kernel, fir_taps=fir_taps),
        in_specs=[SMEM] + [VMEM] * 4,
        out_specs=VMEM,
        out_shape=jax.ShapeDtypeStruct((channels * LAG_WIDTH, samples + LANES), BF16),
        scratch_shapes=[pltpu.VMEM((channels * samples // LANES, LANES), F32)],
        compiler_params=pltpu.CompilerParams(vmem_limit_bytes=32 * MIB),
        cost_estimate=pl.CostEstimate(
            flops=2 * 3 * channels * samples * 3 * LANES, bytes_accessed=10 * channels * samples * 2, transcendentals=0
        ),
        name="shifted_rows",
    )(place, traces, low, high, taps_row)


def correlate(place, parts, shifted, sources, channels, samples):
    blocks = samples // LANES + 2 * EDGE
    rows = sum(part.shape[0] for part in parts)
    scale = 1.0 / math.sqrt(samples)
    return pl.pallas_call(
        functools.partial(
            correlate_kernel,
            sources=sources,
            channels=channels,
            samples=samples,
            pieces=len(parts),
            scale=scale,
        ),
        grid=(channels // GROUP,),
        in_specs=[SMEM] + [VMEM] * len(parts) + [VMEM],
        out_specs=pl.BlockSpec(memory_space=pl.ANY),
        out_shape=jax.ShapeDtypeStruct((sources, channels, 2 * LAG_HALF), F32),
        scratch_shapes=[
            pltpu.VMEM((rows, LANES), F32),
            pltpu.VMEM(((blocks + 1) * sources, LANES), F32),
            pltpu.VMEM((LAG_BLOCKS * PIECES * sources, samples + LANES), BF16),
            pltpu.VMEM((2, LAG_BLOCKS, sources * GROUP, LANES), F32),
            pltpu.SemaphoreType.DMA((2,)),
        ],
        compiler_params=pltpu.CompilerParams(vmem_limit_bytes=48 * MIB),
        name="correlate",
    )(place, *parts, shifted)


def body(traces, fir_taps, source_index):
    channels, samples = traces.shape
    taps = fir_taps.shape[0]
    width = SIDE * LANES
    slabs = lax.axis_size("tm")
    blocks_of = lax.axis_size("chan")
    forward = [(i, i + 1) for i in range(slabs - 1)]
    low = lax.ppermute(traces[:, samples - width :], "tm", forward)
    high = lax.ppermute(traces[:, :width], "tm", [(b, a) for a, b in forward])

    me = lax.axis_index("chan")
    sources = source_index.shape[0]
    owner = source_index // channels
    offset = source_index - owner * channels
    number = jnp.arange(sources)
    same = (owner[:, None] == owner[None, :]) & (number[None, :] < number[:, None])
    rank = jnp.sum(same.astype(jnp.int32), axis=1)
    match = (owner[None, :] == me) & (rank[None, :] == jnp.arange(MAX_OWN, dtype=jnp.int32)[:, None])
    slot_offset = jnp.sum(jnp.where(match, offset[None, :], 0), axis=1)
    place = jnp.stack([lax.axis_index("tm"), jnp.int32(slabs)]).astype(jnp.int32)
    lead = LANES - (taps - 1) // 2
    taps_row = jnp.pad(fir_taps, (lead, 3 * LANES - lead - taps))[None]

    own = source_rows(slot_offset, place, traces, low, high, taps_row, taps)
    shifted = shifted_rows(place, traces, low, high, taps_row, taps)
    if blocks_of == 8:
        def swap(value, distance):
            return lax.ppermute(value, "chan", [(i, i ^ distance) for i in range(blocks_of)])

        z3, z2, z1 = swap(own, 6), swap(own, 4), swap(own, 2)
        y = swap(own, 1)
        column = jnp.concatenate([z1, z2, z3], axis=0)
        other = swap(column, 1)
        parts = [own, y, column, other]
        apart = owner ^ me
        half = apart // 2
        piece = jnp.where(half == 0, apart, 1 + half + 3 * (apart % 2))
    else:
        parts = [lax.all_gather(own, "chan", axis=0, tiled=True)]
        piece = owner
    start = (piece * own.shape[0] + rank).astype(jnp.int32)
    return correlate(start, parts, shifted, sources, channels, samples)[None]


def solution(mesh):
    placed = (P("chan", "tm"), P(), P())
    return jax.shard_map(
        body, mesh=mesh, in_specs=placed, out_specs=P("tm", None, "chan", None), check_vma=False
    )
```

```python
import functools
import math

import jax
import jax.numpy as jnp
from jax import lax
from jax.experimental import pallas as pl
from jax.experimental.pallas import tpu as pltpu
from jax.sharding import PartitionSpec as P

LAG_HALF = 256
NORM_HALF = 64
MAX_OWN = 12
EPSILON = 1e-05

LANES = 128
LAG_WIDTH = 32
PIECES = LANES // LAG_WIDTH
LAG_BLOCKS = 2 * LAG_HALF // LANES
SIDE = 3
EDGE = LAG_HALF // LANES
GROUP = 8
TILE = 256
UNITS = 2
MIB = 2**20
F32 = jnp.float32
BF16 = jnp.bfloat16


def split(value):
    high = value.astype(BF16)
    return high, (value - high.astype(F32)).astype(BF16)


def dot_t(left, right):
    return lax.dot_general(left, right, (((1,), (1,)), ((), ())), preferred_element_type=F32)


def stacked(blocks):
    wide = [
        jnp.concatenate([blocks[b - 1], blocks[b], blocks[b + 1]], axis=1)
        for b in range(1, len(blocks) - 1)
    ]
    return jnp.concatenate(wide, axis=0)


def normalize(blocks, first, last, has_low, has_high, taps_row, fir_taps):
    rows = blocks[0].shape[0]
    row = lax.broadcasted_iota(jnp.int32, (LANES, 3 * LANES), 0)
    lane = lax.broadcasted_iota(jnp.int32, (LANES, 3 * LANES), 1)
    toeplitz = pltpu.roll(jnp.broadcast_to(taps_row, (LANES, 3 * LANES)), 0, 1, stride=1, stride_axis=0)
    taps_high, taps_low = split(toeplitz)
    reach = lane - row - (LANES - NORM_HALF)
    band = jnp.where((reach >= 0) & (reach <= 2 * NORM_HALF), 1.0, 0.0).astype(BF16)
    wide_high, wide_low = [], []
    pairs = [split(block) for block in blocks]
    wide_high = stacked([p[0] for p in pairs])
    wide_low = stacked([p[1] for p in pairs])
    filtered = dot_t(wide_high, taps_high) + dot_t(wide_low, taps_high) + dot_t(wide_high, taps_low)
    inner = []
    for k in range(len(blocks) - 2):
        block = filtered[k * rows : (k + 1) * rows]
        number = first + 1 + k
        if number < 0:
            block = jnp.where(has_low, block, 0.0)
        elif number > last:
            block = jnp.where(has_high, block, 0.0)
        inner.append(block)
    sizes = [split(jnp.abs(block)) for block in inner]
    total = dot_t(stacked([p[0] for p in sizes]), band) + dot_t(stacked([p[1] for p in sizes]), band)
    level = total / (2 * NORM_HALF + 1)
    return [
        block / (EPSILON + level[k * rows : (k + 1) * rows]) for k, block in enumerate(inner[1:-1])
    ]


def source_kernel(offset, place, traces, low, high, taps_row, out, rows_buf, *, fir_taps):
    samples = traces.shape[1]
    own = samples // LANES
    side = low.shape[1]
    rows_buf[...] = jnp.zeros_like(rows_buf)
    for k in range(MAX_OWN):
        at = offset[k]
        rows_buf[k : k + 1, LANES : LANES + side] = low[pl.ds(at, 1), :]
        rows_buf[k : k + 1, LANES + side : LANES + side + samples] = traces[pl.ds(at, 1), :]
        rows_buf[k : k + 1, LANES + side + samples : LANES + 2 * side + samples] = high[pl.ds(at, 1), :]
    count = rows_buf.shape[1] // LANES
    blocks = [rows_buf[:, b * LANES : (b + 1) * LANES] for b in range(count)]
    normed = normalize(
        blocks, -SIDE - 1, own - 1, place[0] > 0, place[0] < place[1] - 1, taps_row[...], fir_taps
    )
    packed = jnp.concatenate([block[:MAX_OWN] for block in normed], axis=0)
    out[...] = packed.astype(BF16)


def shifted_kernel(place, traces, low, high, taps_row, out, rows_buf, *, fir_taps):
    channels, samples = traces.shape
    own = samples // LANES
    side = low.shape[1]
    blocks = [low[:, side - 2 * LANES : side - LANES], low[:, side - LANES :]]
    blocks += [traces[:, b * LANES : (b + 1) * LANES] for b in range(own)]
    blocks += [high[:, :LANES], high[:, LANES : 2 * LANES]]
    normed = normalize(
        blocks, -2, own - 1, place[0] > 0, place[0] < place[1] - 1, taps_row[...], fir_taps
    )
    for b, block in enumerate(normed):
        rows_buf[b * channels : (b + 1) * channels, :] = block
    lane = lax.broadcasted_iota(jnp.int32, (LAG_WIDTH, LANES), 1)
    later = lane >= lax.broadcasted_iota(jnp.int32, (LAG_WIDTH, LANES), 0)

    beyond = samples + LANES
    if out.shape[1] > beyond:
        out[:, beyond:] = jnp.zeros((out.shape[0], out.shape[1] - beyond), BF16)

    @pl.loop(0, channels, unroll=8)
    def _(c):
        before = jnp.zeros((LAG_WIDTH, LANES), F32)
        at = pl.multiple_of(c * LAG_WIDTH, LAG_WIDTH)
        for b in range(own + 1):
            if b < own:
                line = rows_buf[pl.ds(b * channels + c, 1), :]
                turned = pltpu.roll(
                    jnp.broadcast_to(line, (LAG_WIDTH, LANES)), 0, 1, stride=1, stride_axis=0
                )
            else:
                turned = jnp.zeros((LAG_WIDTH, LANES), F32)
            out[pl.ds(at, LAG_WIDTH), b * LANES : (b + 1) * LANES] = jnp.where(
                later, turned, before
            ).astype(BF16)
            before = turned


def correlate_kernel(*refs, sources, **sizes):
    tiles_of = LAG_BLOCKS * PIECES

    def run(*sums):
        split_sums = [sums[m * tiles_of : (m + 1) * tiles_of] for m in range(UNITS)]
        correlate_steps(split_sums, *refs, sources=sources, **sizes)

    pl.run_scoped(
        run, *[pltpu.ACC(m)((sources, TILE), F32) for m in range(UNITS) for _ in range(tiles_of)]
    )


def correlate_steps(sums, place, *refs, sources, channels, samples, pieces, scale):
    parts = refs[:pieces]
    shifted, out, all_rows, lines, windows, ready, sem = refs[pieces:]
    step = pl.program_id(0)
    steps = pl.num_programs(0)
    depth = shifted.shape[1]
    blocks = samples // LANES + 2 * EDGE
    width = GROUP * LAG_WIDTH
    half_of = LAG_BLOCKS // 2

    def sends(pair, halves):
        return [
            pltpu.make_async_copy(
                ready.at[m, q].reshape(sources, GROUP, LANES),
                out.at[:, pl.ds((pair * UNITS + m) * GROUP, GROUP), pl.ds(q * LANES, LANES)],
                sem.at[m, q],
            )
            for m in range(UNITS)
            for q in halves
        ]

    lane = lax.broadcasted_iota(jnp.int32, (sources, LANES), 1)

    def arrange(m, q):
        whole = [pltpu.matmul_pop(sums[m][q * PIECES + p]) for p in range(PIECES)]
        for half in range(width // LANES):
            tiles = [piece[:, half * LANES : (half + 1) * LANES] * scale for piece in whole]
            gap = PIECES // 2
            while gap:
                wide = gap * LAG_WIDTH
                low_half = lax.rem(lane, 2 * wide) < wide
                for p in range(PIECES):
                    if p & gap:
                        continue
                    a, b = tiles[p], tiles[p + gap]
                    tiles[p] = jnp.where(low_half, a, pltpu.roll(b, wide, 1))
                    tiles[p + gap] = jnp.where(low_half, pltpu.roll(a, LANES - wide, 1), b)
                gap //= 2
            for p in range(PIECES):
                ready.at[m, q][pl.ds(half * PIECES + p, sources, stride=GROUP), :] = tiles[p]

    first, second = list(range(half_of)), list(range(half_of, LAG_BLOCKS))

    def chunk(now, before):
        todo = [(m, q) for q in before for m in range(UNITS)]
        count = depth // TILE
        for k in range(count):
            for m in range(UNITS):
                at = pl.multiple_of((step * UNITS + m) * width, width)
                pltpu.matmul_push_rhs(
                    shifted[pl.ds(at, width), k * TILE : (k + 1) * TILE], k % 2, m, transpose=True
                )
            for i, t in enumerate(range(now[0] * PIECES, (now[-1] + 1) * PIECES)):
                left = windows[t * sources : (t + 1) * sources, k * TILE : (k + 1) * TILE]
                for m in range(UNITS):
                    pltpu.matmul_acc_lhs(sums[m][t], left, load_staged_rhs=k % 2 if i == 0 else None)
            if k % 2 and todo:
                arrange(*todo.pop(0))
        while todo:
            arrange(*todo.pop(0))

    @pl.when(step == 0)
    def _():
        start = 0
        for part in parts:
            all_rows[start : start + part.shape[0], :] = part[...].astype(F32)
            start += part.shape[0]
        lines[blocks * sources :, :] = jnp.zeros((sources, LANES), F32)
        windows[:, samples + LANES :] = jnp.zeros((windows.shape[0], depth - samples - LANES), BF16)

        for s in range(sources):
            lines[pl.ds(s, blocks, stride=sources), :] = all_rows[
                pl.ds(place[s], blocks, stride=MAX_OWN), :
            ]

        for p in range(PIECES):
            turn = p * LAG_WIDTH
            turned = None
            for b in range(blocks + 1):
                line = lines[b * sources : (b + 1) * sources, :]
                following = pltpu.roll(line, LANES - turn, 1) if p else line
                if b:
                    block = b - 1
                    value = jnp.where(lane < LANES - turn, turned, following).astype(BF16)
                    for q in range(LAG_BLOCKS):
                        if 0 <= block - q <= samples // LANES:
                            at = (q * PIECES + p) * sources
                            windows[at : at + sources, (block - q) * LANES : (block - q + 1) * LANES] = value
                turned = following

    @pl.when(step >= 2)
    def _():
        for copy in sends(step - 2, second):
            copy.wait()

    chunk(first, second)

    @pl.when(step >= 1)
    def _():
        for copy in sends(step - 1, second):
            copy.start()
        for copy in sends(step - 1, first):
            copy.wait()

    chunk(second, first)
    for copy in sends(step, first):
        copy.start()

    @pl.when(step == steps - 1)
    def _():
        @pl.when(step >= 1)
        def _():
            for copy in sends(step - 1, second):
                copy.wait()

        for q in second:
            for m in range(UNITS):
                arrange(m, q)
        for copy in sends(step, second):
            copy.start()
        for copy in sends(step, first) + sends(step, second):
            copy.wait()


SMEM = pl.BlockSpec(memory_space=pltpu.SMEM)
VMEM = pl.BlockSpec(memory_space=pltpu.VMEM)


def source_rows(offset, place, traces, low, high, taps_row, fir_taps):
    samples = traces.shape[1]
    blocks = samples // LANES + 2 * EDGE
    return pl.pallas_call(
        functools.partial(source_kernel, fir_taps=fir_taps),
        in_specs=[SMEM, SMEM] + [VMEM] * 4,
        out_specs=VMEM,
        out_shape=jax.ShapeDtypeStruct((blocks * MAX_OWN, LANES), BF16),
        scratch_shapes=[pltpu.VMEM((16, samples + 2 * (SIDE + 1) * LANES), F32)],
        compiler_params=pltpu.CompilerParams(vmem_limit_bytes=16 * MIB),
        name="source_rows",
    )(offset, place, traces, low, high, taps_row)


def shifted_rows(place, traces, low, high, taps_row, fir_taps):
    channels, samples = traces.shape
    return pl.pallas_call(
        functools.partial(shifted_kernel, fir_taps=fir_taps),
        in_specs=[SMEM] + [VMEM] * 4,
        out_specs=VMEM,
        out_shape=jax.ShapeDtypeStruct((channels * LAG_WIDTH, -(-(samples + LANES) // TILE) * TILE), BF16),
        scratch_shapes=[pltpu.VMEM((channels * samples // LANES, LANES), F32)],
        compiler_params=pltpu.CompilerParams(vmem_limit_bytes=32 * MIB),
        cost_estimate=pl.CostEstimate(
            flops=2 * 3 * channels * samples * 3 * LANES, bytes_accessed=10 * channels * samples * 2, transcendentals=0
        ),
        name="shifted_rows",
    )(place, traces, low, high, taps_row)


def correlate(place, parts, shifted, sources, channels, samples):
    blocks = samples // LANES + 2 * EDGE
    rows = sum(part.shape[0] for part in parts)
    scale = 1.0 / math.sqrt(samples)
    return pl.pallas_call(
        functools.partial(
            correlate_kernel,
            sources=sources,
            channels=channels,
            samples=samples,
            pieces=len(parts),
            scale=scale,
        ),
        grid=(channels // (UNITS * GROUP),),
        in_specs=[SMEM] + [VMEM] * len(parts) + [VMEM],
        out_specs=pl.BlockSpec(memory_space=pl.ANY),
        out_shape=jax.ShapeDtypeStruct((sources, channels, 2 * LAG_HALF), F32),
        scratch_shapes=[
            pltpu.VMEM((rows, LANES), F32),
            pltpu.VMEM(((blocks + 1) * sources, LANES), F32),
            pltpu.VMEM((LAG_BLOCKS * PIECES * sources, shifted.shape[1]), BF16),
            pltpu.VMEM((UNITS, LAG_BLOCKS, sources * GROUP, LANES), F32),
            pltpu.SemaphoreType.DMA((UNITS, LAG_BLOCKS)),
        ],
        compiler_params=pltpu.CompilerParams(vmem_limit_bytes=24 * MIB),
        name="correlate",
    )(place, *parts, shifted)


def body(traces, fir_taps, source_index):
    channels, samples = traces.shape
    taps = fir_taps.shape[0]
    width = SIDE * LANES
    slabs = lax.axis_size("tm")
    blocks_of = lax.axis_size("chan")
    forward = [(i, i + 1) for i in range(slabs - 1)]
    low = lax.ppermute(traces[:, samples - width :], "tm", forward)
    high = lax.ppermute(traces[:, :width], "tm", [(b, a) for a, b in forward])

    me = lax.axis_index("chan")
    sources = source_index.shape[0]
    owner = source_index // channels
    offset = source_index - owner * channels
    number = jnp.arange(sources)
    same = (owner[:, None] == owner[None, :]) & (number[None, :] < number[:, None])
    rank = jnp.sum(same.astype(jnp.int32), axis=1)
    match = (owner[None, :] == me) & (rank[None, :] == jnp.arange(MAX_OWN, dtype=jnp.int32)[:, None])
    slot_offset = jnp.sum(jnp.where(match, offset[None, :], 0), axis=1)
    place = jnp.stack([lax.axis_index("tm"), jnp.int32(slabs)]).astype(jnp.int32)
    lead = LANES - (taps - 1) // 2
    taps_row = jnp.pad(fir_taps, (lead, 3 * LANES - lead - taps))[None]

    own = source_rows(slot_offset, place, traces, low, high, taps_row, taps)
    shifted = shifted_rows(place, traces, low, high, taps_row, taps)
    if blocks_of == 8:
        def swap(value, distance):
            return lax.ppermute(value, "chan", [(i, i ^ distance) for i in range(blocks_of)])

        z3, z2, z1 = swap(own, 6), swap(own, 4), swap(own, 2)
        y = swap(own, 1)
        column = jnp.concatenate([z1, z2, z3], axis=0)
        other = swap(column, 1)
        parts = [own, y, column, other]
        apart = owner ^ me
        half = apart // 2
        piece = jnp.where(half == 0, apart, 1 + half + 3 * (apart % 2))
    else:
        parts = [lax.all_gather(own, "chan", axis=0, tiled=True)]
        piece = owner
    start = (piece * own.shape[0] + rank).astype(jnp.int32)
    return correlate(start, parts, shifted, sources, channels, samples)[None]


def solution(mesh):
    placed = (P("chan", "tm"), P(), P())
    return jax.shard_map(
        body, mesh=mesh, in_specs=placed, out_specs=P("tm", None, "chan", None), check_vma=False
    )
```

```python
import functools
import math

import jax
import jax.numpy as jnp
from jax import lax
from jax.experimental import pallas as pl
from jax.experimental.pallas import tpu as pltpu
from jax.sharding import PartitionSpec as P

LAG_HALF = 256
NORM_HALF = 64
MAX_OWN = 12
EPSILON = 1e-05

LANES = 128
LAG_WIDTH = 32
PIECES = LANES // LAG_WIDTH
LAG_BLOCKS = 2 * LAG_HALF // LANES
SIDE = 3
EDGE = LAG_HALF // LANES
ROWS = 16
GROUP = 8
TILE = 256
UNITS = 2
EARLY = (1,)
MIB = 2**20
F32 = jnp.float32
BF16 = jnp.bfloat16


def split(value):
    high = value.astype(BF16)
    return high, (value - high.astype(F32)).astype(BF16)


def dot_t(left, right):
    return lax.dot_general(left, right, (((1,), (1,)), ((), ())), preferred_element_type=F32)


def stacked(blocks):
    wide = [
        jnp.concatenate([blocks[b - 1], blocks[b], blocks[b + 1]], axis=1)
        for b in range(1, len(blocks) - 1)
    ]
    return jnp.concatenate(wide, axis=0)


def normalize(pairs, first, last, has_low, has_high, taps_row):
    rows = pairs[0][0].shape[0]
    row = lax.broadcasted_iota(jnp.int32, (LANES, 3 * LANES), 0)
    lane = lax.broadcasted_iota(jnp.int32, (LANES, 3 * LANES), 1)
    toeplitz = pltpu.roll(jnp.broadcast_to(taps_row, (LANES, 3 * LANES)), 0, 1, stride=1, stride_axis=0)
    taps_high, taps_low = split(toeplitz)
    reach = lane - row - (LANES - NORM_HALF)
    band = jnp.where((reach >= 0) & (reach <= 2 * NORM_HALF), 1.0, 0.0).astype(BF16)
    wide_high = stacked([p[0] for p in pairs])
    wide_low = stacked([p[1] for p in pairs])
    filtered = dot_t(wide_high, taps_high) + dot_t(wide_low, taps_high) + dot_t(wide_high, taps_low)
    inner = []
    for k in range(len(pairs) - 2):
        block = filtered[k * rows : (k + 1) * rows]
        number = first + 1 + k
        if number < 0:
            block = jnp.where(has_low, block, 0.0)
        elif number > last:
            block = jnp.where(has_high, block, 0.0)
        inner.append(block)
    sizes = [split(jnp.abs(block)) for block in inner]
    total = dot_t(stacked([p[0] for p in sizes]), band) + dot_t(stacked([p[1] for p in sizes]), band)
    level = total / (2 * NORM_HALF + 1)
    return [
        block / (EPSILON + level[k * rows : (k + 1) * rows]) for k, block in enumerate(inner[1:-1])
    ]


def dot(left, right):
    return jnp.dot(left, right, preferred_element_type=F32)


def pick_kernel(place, index, traces, pick, high, low, rows_high, rows_low):
    channels = traces.shape[0]
    sources = index.shape[1]
    channel = lax.broadcasted_iota(jnp.int32, (channels, sources), 0) + place[3] * channels
    number = lax.broadcasted_iota(jnp.int32, (channels, sources), 1).astype(F32)
    equal = jnp.where(index[...] == channel, 1.0, 0.0)
    here = jnp.sum(equal, axis=1, keepdims=True)
    order = jnp.sum(equal * number, axis=1, keepdims=True)
    across = lax.broadcasted_iota(jnp.int32, (ROWS, sources), 1).astype(F32).astype(BF16)
    here_row = dot_t(jnp.ones((ROWS, sources), BF16), equal.astype(BF16))
    order_row = dot_t(across, equal.astype(BF16))
    rank = jnp.sum(jnp.where(order < order_row[:1], here, 0.0), axis=0, keepdims=True)
    slot = lax.broadcasted_iota(jnp.int32, (ROWS, channels), 0).astype(F32)
    chosen = jnp.where((rank == slot) & (here_row > 0.5), 1.0, 0.0).astype(BF16)
    pick[...] = chosen
    first, second = split(traces[...])
    high[...] = first
    low[...] = second
    rows_high[...] = dot(chosen, first).astype(BF16)
    rows_low[...] = dot(chosen, second).astype(BF16)


def neighbours(place, a, b):
    even = place[2] == 0
    low = jnp.where(place[0] > 0, jnp.where(even, b, a), 0.0)
    high = jnp.where(place[0] < place[1] - 1, jnp.where(even, a, b), 0.0)
    return low, high


def source_kernel(place, pick, rows_high, rows_low, got_a, got_b, taps_row, out):
    own = rows_high.shape[1] // LANES

    def blocks_of(high, low, count):
        return [
            (high[:, b * LANES : (b + 1) * LANES], low[:, b * LANES : (b + 1) * LANES])
            for b in range(count)
        ]

    sides = []
    for edge in neighbours(place, got_a[...], got_b[...]):
        high, low = [dot(pick[...], part).astype(BF16) for part in split(edge)]
        sides.append(blocks_of(high, low, SIDE))
    nothing = jnp.zeros((ROWS, LANES), BF16)
    pairs = [(nothing, nothing)] + sides[0] + blocks_of(rows_high, rows_low, own) + sides[1]
    pairs += [(nothing, nothing)]
    normed = normalize(
        pairs, -SIDE - 1, own - 1, place[0] > 0, place[0] < place[1] - 1, taps_row[...]
    )
    packed = jnp.concatenate([block[:MAX_OWN] for block in normed], axis=0)
    out[...] = packed.astype(BF16)


def normed_kernel(place, index, high, low, got_a, got_b, taps_row, out, start, *, owners, paired):
    channels, samples = high.shape
    own = samples // LANES
    sources = index.shape[1]
    line = jnp.broadcast_to(index[...], (sources, sources))
    ahead = lax.broadcasted_iota(jnp.int32, (sources, sources), 0)
    behind = lax.broadcasted_iota(jnp.int32, (sources, sources), 1)

    def owner_of(value):
        return ((value.astype(F32) + 0.5) * (1.0 / channels)).astype(jnp.int32)

    upright = jnp.sum(jnp.where(ahead == behind, line, 0).astype(F32), axis=1, keepdims=True)
    owner = owner_of(index[...])
    same = (owner_of(upright) == owner) & (ahead < behind)
    rank = jnp.sum(jnp.where(same, 1.0, 0.0), axis=0, keepdims=True).astype(jnp.int32)
    if paired:
        apart = owner ^ place[3]
        piece = lax.shift_right_logical(apart, 1) + (apart & 1) * (owners // 2)
    else:
        piece = owner
    start[...] = piece * (MAX_OWN * (own + 2 * EDGE)) + rank
    before, after = neighbours(place, got_a[...], got_b[...])
    nothing = jnp.zeros((channels, LANES), BF16)
    pairs = [(nothing, nothing), split(before[:, (SIDE - 1) * LANES :])]
    pairs += [
        (high[:, b * LANES : (b + 1) * LANES], low[:, b * LANES : (b + 1) * LANES]) for b in range(own)
    ]
    pairs += [split(after[:, :LANES]), (nothing, nothing)]
    normed = normalize(pairs, -2, own - 1, place[0] > 0, place[0] < place[1] - 1, taps_row[...])
    for b, block in enumerate(normed):
        out[b * channels : (b + 1) * channels, :] = block


def shifted_kernel(normed, out, *, channels):
    own = normed.shape[0] // channels
    lane = lax.broadcasted_iota(jnp.int32, (LAG_WIDTH, LANES), 1)
    later = lane >= lax.broadcasted_iota(jnp.int32, (LAG_WIDTH, LANES), 0)
    beyond = (own + 1) * LANES
    if out.shape[1] > beyond:
        out[:, beyond:] = jnp.zeros((out.shape[0], out.shape[1] - beyond), BF16)

    @pl.loop(0, channels, unroll=8)
    def _(c):
        before = jnp.zeros((LAG_WIDTH, LANES), F32)
        at = pl.multiple_of(c * LAG_WIDTH, LAG_WIDTH)
        for b in range(own + 1):
            if b < own:
                line = normed[pl.ds(b * channels + c, 1), :]
                turned = pltpu.roll(
                    jnp.broadcast_to(line, (LAG_WIDTH, LANES)), 0, 1, stride=1, stride_axis=0
                )
            else:
                turned = jnp.zeros((LAG_WIDTH, LANES), F32)
            out[pl.ds(at, LAG_WIDTH), b * LANES : (b + 1) * LANES] = jnp.where(
                later, turned, before
            ).astype(BF16)
            before = turned


def correlate_kernel(*refs, sources, **sizes):
    tiles_of = LAG_BLOCKS * PIECES

    def run(*sums):
        split_sums = [sums[m * tiles_of : (m + 1) * tiles_of] for m in range(UNITS)]
        correlate_steps(split_sums, *refs, sources=sources, **sizes)

    pl.run_scoped(
        run, *[pltpu.ACC(m)((sources, TILE), F32) for m in range(UNITS) for _ in range(tiles_of)]
    )


def correlate_steps(sums, place, *refs, sources, channels, samples, pieces, scale):
    parts = refs[:pieces]
    shifted, out, all_rows, lines, windows, ready, sem = refs[pieces:]
    step = pl.program_id(0)
    steps = pl.num_programs(0)
    depth = shifted.shape[1]
    blocks = samples // LANES + 2 * EDGE
    width = GROUP * LAG_WIDTH
    half_of = LAG_BLOCKS // 2

    boxes = ready.reshape(sources, UNITS + 1, LAG_BLOCKS + 1, GROUP, LANES)
    spread = (UNITS + 1) * (LAG_BLOCKS + 1) * GROUP

    def send(pair, halves):
        return pltpu.make_async_copy(
            boxes.at[:, 0:UNITS, halves[0] : halves[-1] + 1],
            out.at[:, pl.ds(pair * UNITS, UNITS), halves[0] : halves[-1] + 1],
            sem.at[halves[0] // half_of],
        )

    lane = lax.broadcasted_iota(jnp.int32, (sources, LANES), 1)

    def arrange(m, q):
        whole = [pltpu.matmul_pop(sums[m][q * PIECES + p]) for p in range(PIECES)]
        for half in range(width // LANES):
            tiles = [piece[:, half * LANES : (half + 1) * LANES] * scale for piece in whole]
            gap = PIECES // 2
            while gap:
                wide = gap * LAG_WIDTH
                low_half = lax.rem(lane, 2 * wide) < wide
                for p in range(PIECES):
                    if p & gap:
                        continue
                    a, b = tiles[p], tiles[p + gap]
                    tiles[p] = jnp.where(low_half, a, pltpu.roll(b, wide, 1))
                    tiles[p + gap] = jnp.where(low_half, pltpu.roll(a, LANES - wide, 1), b)
                gap //= 2
            for p in range(PIECES):
                at = (m * (LAG_BLOCKS + 1) + q) * GROUP + half * PIECES + p
                ready[pl.ds(at, sources, stride=spread), :] = tiles[p]

    first, second = list(range(half_of)), list(range(half_of, LAG_BLOCKS))

    def chunk(now, before):
        todo = [(m, q) for q in before for m in range(UNITS)]
        count = depth // TILE
        for k in range(count):
            for m in range(UNITS):
                at = pl.multiple_of((step * UNITS + m) * width, width)
                pltpu.matmul_push_rhs(
                    shifted[pl.ds(at, width), k * TILE : (k + 1) * TILE], k % 2, m, transpose=True
                )
            for i, t in enumerate(range(now[0] * PIECES, (now[-1] + 1) * PIECES)):
                left = windows[t * sources : (t + 1) * sources, k * TILE : (k + 1) * TILE]
                for m in range(UNITS):
                    pltpu.matmul_acc_lhs(sums[m][t], left, load_staged_rhs=k % 2 if i == 0 else None)
            if k % 2 and todo:
                arrange(*todo.pop(0))
        while todo:
            arrange(*todo.pop(0))

    @pl.when(step == 0)
    def _():
        start = 0
        for part in parts:
            all_rows[start : start + part.shape[0], :] = part[...].astype(F32)
            start += part.shape[0]
        lines[blocks * sources :, :] = jnp.zeros((sources, LANES), F32)
        windows[:, samples + LANES :] = jnp.zeros((windows.shape[0], depth - samples - LANES), BF16)

        for s in range(sources):
            lines[pl.ds(s, blocks, stride=sources), :] = all_rows[
                pl.ds(place[0, s], blocks, stride=MAX_OWN), :
            ]

        for p in range(PIECES):
            turn = p * LAG_WIDTH
            turned = None
            for b in range(blocks + 1):
                line = lines[b * sources : (b + 1) * sources, :]
                following = pltpu.roll(line, LANES - turn, 1) if p else line
                if b:
                    block = b - 1
                    value = jnp.where(lane < LANES - turn, turned, following).astype(BF16)
                    for q in range(LAG_BLOCKS):
                        if 0 <= block - q <= samples // LANES:
                            at = (q * PIECES + p) * sources
                            windows[at : at + sources, (block - q) * LANES : (block - q + 1) * LANES] = value
                turned = following

    @pl.when(step >= 2)
    def _():
        send(step - 2, second).wait()

    chunk(first, second)

    @pl.when(step >= 1)
    def _():
        send(step - 1, second).start()
        send(step - 1, first).wait()

    chunk(second, first)
    send(step, first).start()

    @pl.when(step == steps - 1)
    def _():
        @pl.when(step >= 1)
        def _():
            send(step - 1, second).wait()

        for q in second:
            for m in range(UNITS):
                arrange(m, q)
        send(step, second).start()
        send(step, first).wait()
        send(step, second).wait()


SMEM = pl.BlockSpec(memory_space=pltpu.SMEM)
VMEM = pl.BlockSpec(memory_space=pltpu.VMEM)


def picked_rows(place, index, traces):
    channels, samples = traces.shape
    slab = jax.ShapeDtypeStruct(traces.shape, BF16)
    rows = jax.ShapeDtypeStruct((ROWS, samples), BF16)
    return pl.pallas_call(
        pick_kernel,
        in_specs=[SMEM, VMEM, VMEM],
        out_specs=[VMEM] * 5,
        out_shape=[jax.ShapeDtypeStruct((ROWS, channels), BF16), slab, slab, rows, rows],
        compiler_params=pltpu.CompilerParams(vmem_limit_bytes=8 * MIB),
        name="picked_rows",
    )(place, index[None], traces)


def source_rows(place, pick, rows_high, rows_low, got_a, got_b, taps_row):
    blocks = rows_high.shape[1] // LANES + 2 * EDGE
    return pl.pallas_call(
        source_kernel,
        in_specs=[SMEM] + [VMEM] * 6,
        out_specs=VMEM,
        out_shape=jax.ShapeDtypeStruct((blocks * MAX_OWN, LANES), BF16),
        compiler_params=pltpu.CompilerParams(vmem_limit_bytes=8 * MIB),
        name="source_rows",
    )(place, pick, rows_high, rows_low, got_a, got_b, taps_row)


def normed_rows(place, index, high, low, got_a, got_b, taps_row, owners, paired):
    channels, samples = high.shape
    return pl.pallas_call(
        functools.partial(normed_kernel, owners=owners, paired=paired),
        in_specs=[SMEM] + [VMEM] * 6,
        out_specs=[VMEM] * 2,
        out_shape=[
            jax.ShapeDtypeStruct((channels * samples // LANES, LANES), F32),
            jax.ShapeDtypeStruct((1, index.shape[0]), jnp.int32),
        ],
        compiler_params=pltpu.CompilerParams(vmem_limit_bytes=24 * MIB),
        cost_estimate=pl.CostEstimate(
            flops=2 * 5 * channels * samples * 3 * LANES,
            bytes_accessed=16 * channels * samples,
            transcendentals=0,
        ),
        name="normed_rows",
    )(place, index[None], high, low, got_a, got_b, taps_row)


def shifted_rows(normed, channels):
    samples = normed.shape[0] // channels * LANES
    depth = -(-(samples + LANES) // TILE) * TILE
    return pl.pallas_call(
        functools.partial(shifted_kernel, channels=channels),
        in_specs=[VMEM],
        out_specs=VMEM,
        out_shape=jax.ShapeDtypeStruct((channels * LAG_WIDTH, depth), BF16),
        compiler_params=pltpu.CompilerParams(vmem_limit_bytes=4 * MIB),
        cost_estimate=pl.CostEstimate(
            flops=4 * channels * LAG_WIDTH * depth,
            bytes_accessed=2 * channels * LAG_WIDTH * depth,
            transcendentals=0,
        ),
        name="shifted_rows",
    )(normed)


def correlate(place, parts, shifted, sources, channels, samples):
    blocks = samples // LANES + 2 * EDGE
    rows = sum(part.shape[0] for part in parts)
    scale = 1.0 / math.sqrt(samples)
    boxes = pl.pallas_call(
        functools.partial(
            correlate_kernel,
            sources=sources,
            channels=channels,
            samples=samples,
            pieces=len(parts),
            scale=scale,
        ),
        grid=(channels // (UNITS * GROUP),),
        in_specs=[SMEM] + [VMEM] * len(parts) + [VMEM],
        out_specs=pl.BlockSpec(memory_space=pl.ANY),
        out_shape=jax.ShapeDtypeStruct(
            (sources, channels // GROUP, LAG_BLOCKS, GROUP, LANES), F32
        ),
        scratch_shapes=[
            pltpu.VMEM((rows, LANES), F32),
            pltpu.VMEM(((blocks + 1) * sources, LANES), F32),
            pltpu.VMEM((LAG_BLOCKS * PIECES * sources, shifted.shape[1]), BF16),
            pltpu.VMEM((sources * (UNITS + 1) * (LAG_BLOCKS + 1) * GROUP, LANES), F32),
            pltpu.SemaphoreType.DMA((2,)),
        ],
        compiler_params=pltpu.CompilerParams(vmem_limit_bytes=24 * MIB),
        name="correlate",
    )(place, *parts, shifted)
    return boxes.transpose(0, 1, 3, 2, 4).reshape(sources, channels, 2 * LAG_HALF)


def body(traces, fir_taps, source_index):
    channels, samples = traces.shape
    taps = fir_taps.shape[0]
    slabs = lax.axis_size("tm")
    owners = lax.axis_size("chan")
    slab = lax.axis_index("tm")
    in_pairs = slabs % 2 == 0
    parity = slab % 2 if in_pairs else 0 * slab
    place = jnp.stack([slab, jnp.full_like(slab, slabs), parity, lax.axis_index("chan")])
    place = place.astype(jnp.int32)
    lead = LANES - (taps - 1) // 2
    taps_row = jnp.pad(fir_taps, (lead, 3 * LANES - lead - taps))[None]

    left, right = traces[:, : SIDE * LANES], traces[:, samples - SIDE * LANES :]
    if in_pairs:
        edge_a, edge_b = jnp.where(parity == 0, right, left), jnp.where(parity == 0, left, right)
        got_b = lax.ppermute(edge_b, "tm", [(i, (i + 1 if i % 2 else i - 1) % slabs) for i in range(slabs)])
        got_a = lax.ppermute(edge_a, "tm", [(i, i ^ 1) for i in range(slabs)])
    else:
        got_b = lax.ppermute(right, "tm", [(i, i + 1) for i in range(slabs - 1)])
        got_a = lax.ppermute(left, "tm", [(i + 1, i) for i in range(slabs - 1)])
    pick, high, low, *rows = picked_rows(place, source_index, traces)
    own = source_rows(place, pick, *rows, got_a, got_b, taps_row)
    paired = owners in (4, 8)
    normed, start = normed_rows(
        place, source_index, high, low, got_a, got_b, taps_row, owners, paired
    )
    if paired:

        def swap(value, distance):
            return lax.ppermute(value, "chan", [(i, i ^ distance) for i in range(owners)])

        early = [swap(own, distance) for distance in EARLY]
        column = [swap(own, distance) for distance in range(2, owners, 2)]
        held = lax.optimization_barrier((*column, *early, normed))
        column, early, normed = list(held[: len(column)]), list(held[len(column) : -1]), held[-1]
        column = [own] + column
        late = jnp.concatenate(column[len(EARLY) :], axis=0)
        parts = column[: len(EARLY)] + [late] + early + [swap(late, 1)]
    else:
        parts = [lax.all_gather(own, "chan", axis=0, tiled=True)]
    shifted = shifted_rows(normed, channels)
    return correlate(start, parts, shifted, source_index.shape[0], channels, samples)[None]


def solution(mesh):
    placed = (P("chan", "tm"), P(), P())
    return jax.shard_map(
        body, mesh=mesh, in_specs=placed, out_specs=P("tm", None, "chan", None), check_vma=False
    )
```

```python
import functools
import math

import jax
import jax.numpy as jnp
from jax import lax
from jax.experimental import pallas as pl
from jax.experimental.pallas import tpu as pltpu
from jax.sharding import PartitionSpec as P

LAG_HALF = 256
NORM_HALF = 64
MAX_OWN = 12
EPSILON = 1e-05

LANES = 128
LAG_WIDTH = 32
PIECES = LANES // LAG_WIDTH
LAG_BLOCKS = 2 * LAG_HALF // LANES
SIDE = 3
EDGE = LAG_HALF // LANES
ROWS = 16
GROUP = 8
TILE = 256
UNITS = 2
EARLY = (1,)
MIB = 2**20
F32 = jnp.float32
BF16 = jnp.bfloat16


def split(value):
    high = value.astype(BF16)
    return high, (value - high.astype(F32)).astype(BF16)


def dot_t(left, right):
    return lax.dot_general(left, right, (((1,), (1,)), ((), ())), preferred_element_type=F32)


def stacked(blocks):
    wide = [
        jnp.concatenate([blocks[b - 1], blocks[b], blocks[b + 1]], axis=1)
        for b in range(1, len(blocks) - 1)
    ]
    return jnp.concatenate(wide, axis=0)


def normalize(pairs, first, last, has_low, has_high, taps_row):
    rows = pairs[0][0].shape[0]
    row = lax.broadcasted_iota(jnp.int32, (LANES, 3 * LANES), 0)
    lane = lax.broadcasted_iota(jnp.int32, (LANES, 3 * LANES), 1)
    toeplitz = pltpu.roll(jnp.broadcast_to(taps_row, (LANES, 3 * LANES)), 0, 1, stride=1, stride_axis=0)
    taps_high, taps_low = split(toeplitz)
    reach = lane - row - (LANES - NORM_HALF)
    band = jnp.where((reach >= 0) & (reach <= 2 * NORM_HALF), 1.0, 0.0).astype(BF16)
    wide_high = stacked([p[0] for p in pairs])
    wide_low = stacked([p[1] for p in pairs])
    filtered = dot_t(wide_high, taps_high) + dot_t(wide_low, taps_high) + dot_t(wide_high, taps_low)
    inner = []
    for k in range(len(pairs) - 2):
        block = filtered[k * rows : (k + 1) * rows]
        number = first + 1 + k
        if number < 0:
            block = jnp.where(has_low, block, 0.0)
        elif number > last:
            block = jnp.where(has_high, block, 0.0)
        inner.append(block)
    sizes = [split(jnp.abs(block)) for block in inner]
    total = dot_t(stacked([p[0] for p in sizes]), band) + dot_t(stacked([p[1] for p in sizes]), band)
    level = total / (2 * NORM_HALF + 1)
    return [
        block / (EPSILON + level[k * rows : (k + 1) * rows]) for k, block in enumerate(inner[1:-1])
    ]


def dot(left, right):
    return jnp.dot(left, right, preferred_element_type=F32)


def pick_kernel(place, small, traces, pick, high, low, rows_high, rows_low):
    channels = traces.shape[0]
    index = small[:, 3 * LANES :]
    sources = index.shape[1]
    channel = lax.broadcasted_iota(jnp.int32, (channels, sources), 0) + place[3] * channels
    number = lax.broadcasted_iota(jnp.int32, (channels, sources), 1).astype(F32)
    equal = jnp.where(index == channel.astype(F32), 1.0, 0.0)
    here = jnp.sum(equal, axis=1, keepdims=True)
    order = jnp.sum(equal * number, axis=1, keepdims=True)
    across = lax.broadcasted_iota(jnp.int32, (ROWS, sources), 1).astype(F32).astype(BF16)
    here_row = dot_t(jnp.ones((ROWS, sources), BF16), equal.astype(BF16))
    order_row = dot_t(across, equal.astype(BF16))
    rank = jnp.sum(jnp.where(order < order_row[:1], here, 0.0), axis=0, keepdims=True)
    slot = lax.broadcasted_iota(jnp.int32, (ROWS, channels), 0).astype(F32)
    chosen = jnp.where((rank == slot) & (here_row > 0.5), 1.0, 0.0).astype(BF16)
    pick[...] = chosen
    first, second = split(traces[...])
    high[...] = first
    low[...] = second
    rows_high[...] = dot(chosen, first).astype(BF16)
    rows_low[...] = dot(chosen, second).astype(BF16)


def neighbours(place, a, b):
    even = place[2] == 0
    low = jnp.where(place[0] > 0, jnp.where(even, b, a), 0.0)
    high = jnp.where(place[0] < place[1] - 1, jnp.where(even, a, b), 0.0)
    return low, high


def source_kernel(place, pick, rows_high, rows_low, got_a, got_b, small, out):
    own = rows_high.shape[1] // LANES

    def blocks_of(high, low, count):
        return [
            (high[:, b * LANES : (b + 1) * LANES], low[:, b * LANES : (b + 1) * LANES])
            for b in range(count)
        ]

    sides = []
    for edge in neighbours(place, got_a[...], got_b[...]):
        high, low = [dot(pick[...], part).astype(BF16) for part in split(edge)]
        sides.append(blocks_of(high, low, SIDE))
    nothing = jnp.zeros((ROWS, LANES), BF16)
    pairs = [(nothing, nothing)] + sides[0] + blocks_of(rows_high, rows_low, own) + sides[1]
    pairs += [(nothing, nothing)]
    normed = normalize(
        pairs, -SIDE - 1, own - 1, place[0] > 0, place[0] < place[1] - 1, small[:, : 3 * LANES]
    )
    packed = jnp.concatenate([block[:MAX_OWN] for block in normed], axis=0)
    out[...] = packed.astype(BF16)


def normed_kernel(place, high, low, got_a, got_b, small, out, start, *, owners, paired):
    channels, samples = high.shape
    own = samples // LANES
    index = small[:, 3 * LANES :]
    sources = index.shape[1]
    line = jnp.broadcast_to(index, (sources, sources))
    ahead = lax.broadcasted_iota(jnp.int32, (sources, sources), 0)
    behind = lax.broadcasted_iota(jnp.int32, (sources, sources), 1)

    def owner_of(value):
        return ((value + 0.5) * (1.0 / channels)).astype(jnp.int32)

    upright = jnp.sum(jnp.where(ahead == behind, line, 0.0), axis=1, keepdims=True)
    owner = owner_of(index)
    same = (owner_of(upright) == owner) & (ahead < behind)
    rank = jnp.sum(jnp.where(same, 1.0, 0.0), axis=0, keepdims=True).astype(jnp.int32)
    if paired:
        apart = owner ^ place[3]
        piece = lax.shift_right_logical(apart, 1) + (apart & 1) * (owners // 2)
    else:
        piece = owner
    start[...] = piece * (MAX_OWN * (own + 2 * EDGE)) + rank
    before, after = neighbours(place, got_a[...], got_b[...])
    nothing = jnp.zeros((channels, LANES), BF16)
    pairs = [(nothing, nothing), split(before[:, (SIDE - 1) * LANES :])]
    pairs += [
        (high[:, b * LANES : (b + 1) * LANES], low[:, b * LANES : (b + 1) * LANES]) for b in range(own)
    ]
    pairs += [split(after[:, :LANES]), (nothing, nothing)]
    normed = normalize(pairs, -2, own - 1, place[0] > 0, place[0] < place[1] - 1, small[:, : 3 * LANES])
    for b, block in enumerate(normed):
        out[b * channels : (b + 1) * channels, :] = block


def shifted_kernel(normed, out, *, channels):
    own = normed.shape[0] // channels
    lane = lax.broadcasted_iota(jnp.int32, (LAG_WIDTH, LANES), 1)
    later = lane >= lax.broadcasted_iota(jnp.int32, (LAG_WIDTH, LANES), 0)
    beyond = (own + 1) * LANES
    if out.shape[1] > beyond:
        out[:, beyond:] = jnp.zeros((out.shape[0], out.shape[1] - beyond), BF16)

    @pl.loop(0, channels, unroll=8)
    def _(c):
        before = jnp.zeros((LAG_WIDTH, LANES), F32)
        at = pl.multiple_of(c * LAG_WIDTH, LAG_WIDTH)
        for b in range(own + 1):
            if b < own:
                line = normed[pl.ds(b * channels + c, 1), :]
                turned = pltpu.roll(
                    jnp.broadcast_to(line, (LAG_WIDTH, LANES)), 0, 1, stride=1, stride_axis=0
                )
            else:
                turned = jnp.zeros((LAG_WIDTH, LANES), F32)
            out[pl.ds(at, LAG_WIDTH), b * LANES : (b + 1) * LANES] = jnp.where(
                later, turned, before
            ).astype(BF16)
            before = turned


def correlate_kernel(*refs, sources, **sizes):
    tiles_of = LAG_BLOCKS * PIECES

    def run(*sums):
        split_sums = [sums[m * tiles_of : (m + 1) * tiles_of] for m in range(UNITS)]
        correlate_steps(split_sums, *refs, sources=sources, **sizes)

    pl.run_scoped(
        run, *[pltpu.ACC(m)((sources, TILE), F32) for m in range(UNITS) for _ in range(tiles_of)]
    )


def correlate_steps(sums, place, *refs, sources, channels, samples, pieces, scale):
    parts = refs[:pieces]
    shifted, out, all_rows, lines, windows, ready, sem = refs[pieces:]
    step = pl.program_id(0)
    steps = pl.num_programs(0)
    depth = shifted.shape[1]
    blocks = samples // LANES + 2 * EDGE
    width = GROUP * LAG_WIDTH
    half_of = LAG_BLOCKS // 2

    boxes = ready.reshape(sources, UNITS + 1, LAG_BLOCKS + 1, GROUP, LANES)
    spread = (UNITS + 1) * (LAG_BLOCKS + 1) * GROUP

    def send(pair, halves):
        return pltpu.make_async_copy(
            boxes.at[:, 0:UNITS, halves[0] : halves[-1] + 1],
            out.at[:, pl.ds(pair * UNITS, UNITS), halves[0] : halves[-1] + 1],
            sem.at[halves[0] // half_of],
        )

    def unit(m, q, which):
        return pltpu.make_async_copy(
            boxes.at[:, m, q], out.at[:, step * UNITS + m, q], sem.at[2 + which]
        )

    lane = lax.broadcasted_iota(jnp.int32, (sources, LANES), 1)

    def arrange(m, q):
        whole = [pltpu.matmul_pop(sums[m][q * PIECES + p]) for p in range(PIECES)]
        for half in range(width // LANES):
            tiles = [piece[:, half * LANES : (half + 1) * LANES] * scale for piece in whole]
            gap = PIECES // 2
            while gap:
                wide = gap * LAG_WIDTH
                low_half = lax.rem(lane, 2 * wide) < wide
                for p in range(PIECES):
                    if p & gap:
                        continue
                    a, b = tiles[p], tiles[p + gap]
                    tiles[p] = jnp.where(low_half, a, pltpu.roll(b, wide, 1))
                    tiles[p + gap] = jnp.where(low_half, pltpu.roll(a, LANES - wide, 1), b)
                gap //= 2
            for p in range(PIECES):
                at = (m * (LAG_BLOCKS + 1) + q) * GROUP + half * PIECES + p
                ready[pl.ds(at, sources, stride=spread), :] = tiles[p]

    first, second = list(range(half_of)), list(range(half_of, LAG_BLOCKS))

    def chunk(now, before):
        todo = [(m, q) for q in before for m in range(UNITS)]
        count = depth // TILE
        for k in range(count):
            for m in range(UNITS):
                at = pl.multiple_of((step * UNITS + m) * width, width)
                pltpu.matmul_push_rhs(
                    shifted[pl.ds(at, width), k * TILE : (k + 1) * TILE], k % 2, m, transpose=True
                )
            for i, t in enumerate(range(now[0] * PIECES, (now[-1] + 1) * PIECES)):
                left = windows[t * sources : (t + 1) * sources, k * TILE : (k + 1) * TILE]
                for m in range(UNITS):
                    pltpu.matmul_acc_lhs(sums[m][t], left, load_staged_rhs=k % 2 if i == 0 else None)
            if k % 2 and todo:
                arrange(*todo.pop(0))
        while todo:
            arrange(*todo.pop(0))

    @pl.when(step == 0)
    def _():
        start = 0
        for part in parts:
            all_rows[start : start + part.shape[0], :] = part[...].astype(F32)
            start += part.shape[0]
        pitch = sources + 8
        lines[blocks * pitch : blocks * pitch + sources, :] = jnp.zeros((sources, LANES), F32)
        windows[:, samples + LANES :] = jnp.zeros((windows.shape[0], depth - samples - LANES), BF16)

        for s in range(sources):
            lines[pl.ds(s, blocks, stride=pitch), :] = all_rows[
                pl.ds(place[0, s], blocks, stride=MAX_OWN), :
            ]

        for p in range(PIECES):
            turn = p * LAG_WIDTH
            turned = None
            for b in range(blocks + 1):
                line = lines[b * pitch : b * pitch + sources, :]
                following = pltpu.roll(line, LANES - turn, 1) if p else line
                if b:
                    block = b - 1
                    value = jnp.where(lane < LANES - turn, turned, following).astype(BF16)
                    for q in range(LAG_BLOCKS):
                        if 0 <= block - q <= samples // LANES:
                            at = (q * PIECES + p) * sources
                            windows[at : at + sources, (block - q) * LANES : (block - q + 1) * LANES] = value
                turned = following

    @pl.when(step >= 2)
    def _():
        send(step - 2, second).wait()

    chunk(first, second)

    @pl.when(step >= 1)
    def _():
        send(step - 1, second).start()
        send(step - 1, first).wait()

    chunk(second, first)
    send(step, first).start()

    @pl.when(step == steps - 1)
    def _():
        @pl.when(step >= 1)
        def _():
            send(step - 1, second).wait()

        left = [(m, q) for q in second for m in range(UNITS)]
        for i, (m, q) in enumerate(left):
            arrange(m, q)
            unit(m, q, i).start()
        send(step, first).wait()
        for i, (m, q) in enumerate(left):
            unit(m, q, i).wait()


SMEM = pl.BlockSpec(memory_space=pltpu.SMEM)
VMEM = pl.BlockSpec(memory_space=pltpu.VMEM)


def picked_rows(place, small, traces):
    channels, samples = traces.shape
    slab = jax.ShapeDtypeStruct(traces.shape, BF16)
    rows = jax.ShapeDtypeStruct((ROWS, samples), BF16)
    return pl.pallas_call(
        pick_kernel,
        in_specs=[SMEM, VMEM, VMEM],
        out_specs=[VMEM] * 5,
        out_shape=[jax.ShapeDtypeStruct((ROWS, channels), BF16), slab, slab, rows, rows],
        compiler_params=pltpu.CompilerParams(vmem_limit_bytes=8 * MIB),
        name="picked_rows",
    )(place, small, traces)


def source_rows(place, pick, rows_high, rows_low, got_a, got_b, small):
    blocks = rows_high.shape[1] // LANES + 2 * EDGE
    return pl.pallas_call(
        source_kernel,
        in_specs=[SMEM] + [VMEM] * 6,
        out_specs=VMEM,
        out_shape=jax.ShapeDtypeStruct((blocks * MAX_OWN, LANES), BF16),
        compiler_params=pltpu.CompilerParams(vmem_limit_bytes=8 * MIB),
        name="source_rows",
    )(place, pick, rows_high, rows_low, got_a, got_b, small)


def normed_rows(place, small, high, low, got_a, got_b, owners, paired):
    channels, samples = high.shape
    return pl.pallas_call(
        functools.partial(normed_kernel, owners=owners, paired=paired),
        in_specs=[SMEM] + [VMEM] * 5,
        out_specs=[VMEM] * 2,
        out_shape=[
            jax.ShapeDtypeStruct((channels * samples // LANES, LANES), F32),
            jax.ShapeDtypeStruct((1, small.shape[1] - 3 * LANES), jnp.int32),
        ],
        compiler_params=pltpu.CompilerParams(vmem_limit_bytes=24 * MIB),
        cost_estimate=pl.CostEstimate(
            flops=2 * 5 * channels * samples * 3 * LANES,
            bytes_accessed=16 * channels * samples,
            transcendentals=0,
        ),
        name="normed_rows",
    )(place, high, low, got_a, got_b, small)


def shifted_rows(normed, channels):
    samples = normed.shape[0] // channels * LANES
    depth = -(-(samples + LANES) // TILE) * TILE
    return pl.pallas_call(
        functools.partial(shifted_kernel, channels=channels),
        in_specs=[VMEM],
        out_specs=VMEM,
        out_shape=jax.ShapeDtypeStruct((channels * LAG_WIDTH, depth), BF16),
        compiler_params=pltpu.CompilerParams(vmem_limit_bytes=4 * MIB),
        cost_estimate=pl.CostEstimate(
            flops=4 * channels * LAG_WIDTH * depth,
            bytes_accessed=2 * channels * LAG_WIDTH * depth,
            transcendentals=0,
        ),
        name="shifted_rows",
    )(normed)


def correlate(place, parts, shifted, sources, channels, samples):
    blocks = samples // LANES + 2 * EDGE
    rows = sum(part.shape[0] for part in parts)
    scale = 1.0 / math.sqrt(samples)
    boxes = pl.pallas_call(
        functools.partial(
            correlate_kernel,
            sources=sources,
            channels=channels,
            samples=samples,
            pieces=len(parts),
            scale=scale,
        ),
        grid=(channels // (UNITS * GROUP),),
        in_specs=[SMEM] + [VMEM] * len(parts) + [VMEM],
        out_specs=pl.BlockSpec(memory_space=pl.ANY),
        out_shape=jax.ShapeDtypeStruct(
            (sources, channels // GROUP, LAG_BLOCKS, GROUP, LANES), F32
        ),
        scratch_shapes=[
            pltpu.VMEM((rows, LANES), F32),
            pltpu.VMEM(((blocks + 1) * (sources + 8), LANES), F32),
            pltpu.VMEM((LAG_BLOCKS * PIECES * sources, shifted.shape[1]), BF16),
            pltpu.VMEM((sources * (UNITS + 1) * (LAG_BLOCKS + 1) * GROUP, LANES), F32),
            pltpu.SemaphoreType.DMA((2 + UNITS * LAG_BLOCKS // 2,)),
        ],
        compiler_params=pltpu.CompilerParams(vmem_limit_bytes=24 * MIB),
        name="correlate",
    )(place, *parts, shifted)
    return boxes.transpose(0, 1, 3, 2, 4).reshape(sources, channels, 2 * LAG_HALF)


def body(traces, fir_taps, source_index):
    channels, samples = traces.shape
    taps = fir_taps.shape[0]
    slabs = lax.axis_size("tm")
    owners = lax.axis_size("chan")
    slab = lax.axis_index("tm")
    in_pairs = slabs % 2 == 0
    parity = slab % 2 if in_pairs else 0 * slab
    place = jnp.stack([slab, jnp.full_like(slab, slabs), parity, lax.axis_index("chan")])
    place = place.astype(jnp.int32)
    lead = LANES - (taps - 1) // 2
    total = 3 * LANES + source_index.shape[0]
    small = jnp.pad(fir_taps[None], ((0, 0), (lead, total - lead - taps)))
    small = small + jnp.pad(source_index[None].astype(F32), ((0, 0), (3 * LANES, 0)))

    left, right = traces[:, : SIDE * LANES], traces[:, samples - SIDE * LANES :]
    if in_pairs:
        edge_a, edge_b = jnp.where(parity == 0, right, left), jnp.where(parity == 0, left, right)
        got_b = lax.ppermute(edge_b, "tm", [(i, (i + 1 if i % 2 else i - 1) % slabs) for i in range(slabs)])
        got_a = lax.ppermute(edge_a, "tm", [(i, i ^ 1) for i in range(slabs)])
    else:
        got_b = lax.ppermute(right, "tm", [(i, i + 1) for i in range(slabs - 1)])
        got_a = lax.ppermute(left, "tm", [(i + 1, i) for i in range(slabs - 1)])
    pick, high, low, *rows = picked_rows(place, small, traces)
    own = source_rows(place, pick, *rows, got_a, got_b, small)
    paired = owners in (4, 8)
    normed, start = normed_rows(place, small, high, low, got_a, got_b, owners, paired)
    if paired:

        def swap(value, distance):
            return lax.ppermute(value, "chan", [(i, i ^ distance) for i in range(owners)])

        early = [swap(own, distance) for distance in EARLY]
        column = [swap(own, distance) for distance in range(2, owners, 2)]
        held = lax.optimization_barrier((*column, *early, normed))
        column, early, normed = list(held[: len(column)]), list(held[len(column) : -1]), held[-1]
        column = [own] + column
        late = jnp.concatenate(column[len(EARLY) :], axis=0)
        parts = column[: len(EARLY)] + [late] + early + [swap(late, 1)]
    else:
        parts = [lax.all_gather(own, "chan", axis=0, tiled=True)]
    shifted = shifted_rows(normed, channels)
    return correlate(start, parts, shifted, source_index.shape[0], channels, samples)[None]


def solution(mesh):
    placed = (P("chan", "tm"), P(), P())
    return jax.shard_map(
        body, mesh=mesh, in_specs=placed, out_specs=P("tm", None, "chan", None), check_vma=False
    )
```

```python
import functools
import math

import jax
import jax.numpy as jnp
from jax import lax
from jax.experimental import pallas as pl
from jax.experimental.pallas import tpu as pltpu
from jax.sharding import PartitionSpec as P

LAG_HALF = 256
NORM_HALF = 64
MAX_OWN = 12
EPSILON = 1e-05

LANES = 128
LAG_WIDTH = 32
PIECES = LANES // LAG_WIDTH
LAG_BLOCKS = 2 * LAG_HALF // LANES
SIDE = 3
EDGE = LAG_HALF // LANES
ROWS = 16
GROUP = 8
TILE = 256
UNITS = 2
EARLY = (1,)
MIB = 2**20
F32 = jnp.float32
BF16 = jnp.bfloat16


def split(value):
    high = value.astype(BF16)
    return high, (value - high.astype(F32)).astype(BF16)


def dot_t(left, right):
    return lax.dot_general(left, right, (((1,), (1,)), ((), ())), preferred_element_type=F32)


def stacked(blocks):
    wide = [
        jnp.concatenate([blocks[b - 1], blocks[b], blocks[b + 1]], axis=1)
        for b in range(1, len(blocks) - 1)
    ]
    return jnp.concatenate(wide, axis=0)


def normalize(pairs, first, last, has_low, has_high, taps_row):
    rows = pairs[0][0].shape[0]
    row = lax.broadcasted_iota(jnp.int32, (LANES, 3 * LANES), 0)
    lane = lax.broadcasted_iota(jnp.int32, (LANES, 3 * LANES), 1)
    toeplitz = pltpu.roll(jnp.broadcast_to(taps_row, (LANES, 3 * LANES)), 0, 1, stride=1, stride_axis=0)
    taps_high, taps_low = split(toeplitz)
    reach = lane - row - (LANES - NORM_HALF)
    band = jnp.where((reach >= 0) & (reach <= 2 * NORM_HALF), 1.0, 0.0).astype(BF16)
    wide_high = stacked([p[0] for p in pairs])
    wide_low = stacked([p[1] for p in pairs])
    filtered = dot_t(wide_high, taps_high) + dot_t(wide_low, taps_high) + dot_t(wide_high, taps_low)
    inner = []
    for k in range(len(pairs) - 2):
        block = filtered[k * rows : (k + 1) * rows]
        number = first + 1 + k
        if number < 0:
            block = jnp.where(has_low, block, 0.0)
        elif number > last:
            block = jnp.where(has_high, block, 0.0)
        inner.append(block)
    sizes = [split(jnp.abs(block)) for block in inner]
    total = dot_t(stacked([p[0] for p in sizes]), band) + dot_t(stacked([p[1] for p in sizes]), band)
    level = total / (2 * NORM_HALF + 1)
    return [
        block / (EPSILON + level[k * rows : (k + 1) * rows]) for k, block in enumerate(inner[1:-1])
    ]


def dot(left, right):
    return jnp.dot(left, right, preferred_element_type=F32)


def pick_kernel(place, small, traces, pick, high, low, rows_high, rows_low):
    channels = traces.shape[0]
    index = small[:, 3 * LANES :]
    sources = index.shape[1]
    channel = lax.broadcasted_iota(jnp.int32, (channels, sources), 0) + place[3] * channels
    number = lax.broadcasted_iota(jnp.int32, (channels, sources), 1).astype(F32)
    equal = jnp.where(index == channel.astype(F32), 1.0, 0.0)
    here = jnp.sum(equal, axis=1, keepdims=True)
    order = jnp.sum(equal * number, axis=1, keepdims=True)
    across = lax.broadcasted_iota(jnp.int32, (ROWS, sources), 1).astype(F32).astype(BF16)
    here_row = dot_t(jnp.ones((ROWS, sources), BF16), equal.astype(BF16))
    order_row = dot_t(across, equal.astype(BF16))
    rank = jnp.sum(jnp.where(order < order_row[:1], here, 0.0), axis=0, keepdims=True)
    slot = lax.broadcasted_iota(jnp.int32, (ROWS, channels), 0).astype(F32)
    chosen = jnp.where((rank == slot) & (here_row > 0.5), 1.0, 0.0).astype(BF16)
    pick[...] = chosen
    first, second = split(traces[...])
    high[...] = first
    low[...] = second
    rows_high[...] = dot(chosen, first).astype(BF16)
    rows_low[...] = dot(chosen, second).astype(BF16)


def neighbours(place, a, b):
    even = place[2] == 0
    low = jnp.where(place[0] > 0, jnp.where(even, b, a), 0.0)
    high = jnp.where(place[0] < place[1] - 1, jnp.where(even, a, b), 0.0)
    return low, high


def source_kernel(place, pick, rows_high, rows_low, got_a, got_b, small, out):
    own = rows_high.shape[1] // LANES

    def blocks_of(high, low, count):
        return [
            (high[:, b * LANES : (b + 1) * LANES], low[:, b * LANES : (b + 1) * LANES])
            for b in range(count)
        ]

    sides = []
    for edge in neighbours(place, got_a[...], got_b[...]):
        high, low = [dot(pick[...], part).astype(BF16) for part in split(edge)]
        sides.append(blocks_of(high, low, SIDE))
    nothing = jnp.zeros((ROWS, LANES), BF16)
    pairs = [(nothing, nothing)] + sides[0] + blocks_of(rows_high, rows_low, own) + sides[1]
    pairs += [(nothing, nothing)]
    normed = normalize(
        pairs, -SIDE - 1, own - 1, place[0] > 0, place[0] < place[1] - 1, small[:, : 3 * LANES]
    )
    packed = jnp.concatenate([block[:MAX_OWN] for block in normed], axis=0)
    out[...] = packed.astype(BF16)


def normed_kernel(place, high, low, got_a, got_b, small, out, start, *, owners, paired):
    channels, samples = high.shape
    own = samples // LANES
    index = small[:, 3 * LANES :]
    sources = index.shape[1]
    line = jnp.broadcast_to(index, (sources, sources))
    ahead = lax.broadcasted_iota(jnp.int32, (sources, sources), 0)
    behind = lax.broadcasted_iota(jnp.int32, (sources, sources), 1)

    def owner_of(value):
        return ((value + 0.5) * (1.0 / channels)).astype(jnp.int32)

    upright = jnp.sum(jnp.where(ahead == behind, line, 0.0), axis=1, keepdims=True)
    owner = owner_of(index)
    same = (owner_of(upright) == owner) & (ahead < behind)
    rank = jnp.sum(jnp.where(same, 1.0, 0.0), axis=0, keepdims=True).astype(jnp.int32)
    if paired:
        apart = owner ^ place[3]
        piece = lax.shift_right_logical(apart, 1) + (apart & 1) * (owners // 2)
    else:
        piece = owner
    start[...] = piece * (MAX_OWN * (own + 2 * EDGE)) + rank
    before, after = neighbours(place, got_a[...], got_b[...])
    nothing = jnp.zeros((channels, LANES), BF16)
    pairs = [(nothing, nothing), split(before[:, (SIDE - 1) * LANES :])]
    pairs += [
        (high[:, b * LANES : (b + 1) * LANES], low[:, b * LANES : (b + 1) * LANES]) for b in range(own)
    ]
    pairs += [split(after[:, :LANES]), (nothing, nothing)]
    normed = normalize(pairs, -2, own - 1, place[0] > 0, place[0] < place[1] - 1, small[:, : 3 * LANES])
    for b, block in enumerate(normed):
        out[b * channels : (b + 1) * channels, :] = block


def shifted_kernel(normed, out, *, channels):
    own = normed.shape[0] // channels
    lane = lax.broadcasted_iota(jnp.int32, (LAG_WIDTH, LANES), 1)
    later = lane >= lax.broadcasted_iota(jnp.int32, (LAG_WIDTH, LANES), 0)
    beyond = (own + 1) * LANES
    if out.shape[1] > beyond:
        out[:, beyond:] = jnp.zeros((out.shape[0], out.shape[1] - beyond), BF16)

    @pl.loop(0, channels, unroll=8)
    def _(c):
        before = jnp.zeros((LAG_WIDTH, LANES), F32)
        at = pl.multiple_of(c * LAG_WIDTH, LAG_WIDTH)
        for b in range(own + 1):
            if b < own:
                line = normed[pl.ds(b * channels + c, 1), :]
                turned = pltpu.roll(
                    jnp.broadcast_to(line, (LAG_WIDTH, LANES)), 0, 1, stride=1, stride_axis=0
                )
            else:
                turned = jnp.zeros((LAG_WIDTH, LANES), F32)
            out[pl.ds(at, LAG_WIDTH), b * LANES : (b + 1) * LANES] = jnp.where(
                later, turned, before
            ).astype(BF16)
            before = turned


def correlate_kernel(*refs, sources, **sizes):
    tiles_of = LAG_BLOCKS * PIECES

    def run(*sums):
        split_sums = [sums[m * tiles_of : (m + 1) * tiles_of] for m in range(UNITS)]
        correlate_steps(split_sums, *refs, sources=sources, **sizes)

    pl.run_scoped(
        run, *[pltpu.ACC(m)((sources, TILE), F32) for m in range(UNITS) for _ in range(tiles_of)]
    )


def correlate_steps(sums, place, *refs, sources, channels, samples, pieces, scale):
    parts = refs[:pieces]
    shifted, out, all_rows, lines, windows, ready, sem = refs[pieces:]
    step = pl.program_id(0)
    steps = pl.num_programs(0)
    depth = shifted.shape[1]
    blocks = samples // LANES + 2 * EDGE
    width = GROUP * LAG_WIDTH
    half_of = LAG_BLOCKS // 2

    boxes = ready.reshape(sources, UNITS + 1, LAG_BLOCKS + 1, GROUP, LANES)
    spread = (UNITS + 1) * (LAG_BLOCKS + 1) * GROUP

    def send(pair, halves):
        return pltpu.make_async_copy(
            boxes.at[:, 0:UNITS, halves[0] : halves[-1] + 1],
            out.at[:, pl.ds(pair * UNITS, UNITS), halves[0] : halves[-1] + 1],
            sem.at[halves[0] // half_of],
        )

    def unit(m, q, which):
        return pltpu.make_async_copy(
            boxes.at[:, m, q], out.at[:, step * UNITS + m, q], sem.at[2 + which]
        )

    lane = lax.broadcasted_iota(jnp.int32, (sources, LANES), 1)

    def arrange(m, q):
        whole = [pltpu.matmul_pop(sums[m][q * PIECES + p]) for p in range(PIECES)]
        for half in range(width // LANES):
            tiles = [piece[:, half * LANES : (half + 1) * LANES] * scale for piece in whole]
            gap = PIECES // 2
            while gap:
                wide = gap * LAG_WIDTH
                low_half = lax.rem(lane, 2 * wide) < wide
                for p in range(PIECES):
                    if p & gap:
                        continue
                    a, b = tiles[p], tiles[p + gap]
                    tiles[p] = jnp.where(low_half, a, pltpu.roll(b, wide, 1))
                    tiles[p + gap] = jnp.where(low_half, pltpu.roll(a, LANES - wide, 1), b)
                gap //= 2
            for p in range(PIECES):
                at = (m * (LAG_BLOCKS + 1) + q) * GROUP + half * PIECES + p
                ready[pl.ds(at, sources, stride=spread), :] = tiles[p]

    first, second = list(range(half_of)), list(range(half_of, LAG_BLOCKS))

    def chunk(now, before):
        todo = [(m, q) for q in before for m in range(UNITS)]
        count = depth // TILE
        for k in range(count):
            for m in range(UNITS):
                at = pl.multiple_of((step * UNITS + m) * width, width)
                pltpu.matmul_push_rhs(
                    shifted[pl.ds(at, width), k * TILE : (k + 1) * TILE], k % 2, m, transpose=True
                )
            for i, t in enumerate(range(now[0] * PIECES, (now[-1] + 1) * PIECES)):
                left = windows[t * sources : (t + 1) * sources, k * TILE : (k + 1) * TILE]
                for m in range(UNITS):
                    pltpu.matmul_acc_lhs(sums[m][t], left, load_staged_rhs=k % 2 if i == 0 else None)
            if k % 2 and todo:
                arrange(*todo.pop(0))
        while todo:
            arrange(*todo.pop(0))

    @pl.when(step == 0)
    def _():
        start = 0
        for part in parts:
            all_rows[start : start + part.shape[0], :] = part[...].astype(F32)
            start += part.shape[0]
        pitch = sources + 8
        lines[blocks * pitch : blocks * pitch + sources, :] = jnp.zeros((sources, LANES), F32)
        windows[:, samples + LANES :] = jnp.zeros((windows.shape[0], depth - samples - LANES), BF16)

        for s in range(sources):
            lines[pl.ds(s, blocks, stride=pitch), :] = all_rows[
                pl.ds(place[0, s], blocks, stride=MAX_OWN), :
            ]

        for p in range(PIECES):
            turn = p * LAG_WIDTH
            turned = None
            for b in range(blocks + 1):
                line = lines[b * pitch : b * pitch + sources, :]
                following = pltpu.roll(line, LANES - turn, 1) if p else line
                if b:
                    block = b - 1
                    value = jnp.where(lane < LANES - turn, turned, following).astype(BF16)
                    for q in range(LAG_BLOCKS):
                        if 0 <= block - q <= samples // LANES:
                            at = (q * PIECES + p) * sources
                            windows[at : at + sources, (block - q) * LANES : (block - q + 1) * LANES] = value
                turned = following

    @pl.when(step >= 2)
    def _():
        send(step - 2, second).wait()

    chunk(first, second)

    @pl.when(step >= 1)
    def _():
        send(step - 1, second).start()
        send(step - 1, first).wait()

    chunk(second, first)
    send(step, first).start()

    @pl.when(step == steps - 1)
    def _():
        @pl.when(step >= 1)
        def _():
            send(step - 1, second).wait()

        left = [(m, q) for q in second for m in range(UNITS)]
        for i, (m, q) in enumerate(left):
            arrange(m, q)
            unit(m, q, i).start()
        send(step, first).wait()
        for i, (m, q) in enumerate(left):
            unit(m, q, i).wait()


SMEM = pl.BlockSpec(memory_space=pltpu.SMEM)
VMEM = pl.BlockSpec(memory_space=pltpu.VMEM)


def picked_rows(place, small, traces):
    channels, samples = traces.shape
    slab = jax.ShapeDtypeStruct(traces.shape, BF16)
    rows = jax.ShapeDtypeStruct((ROWS, samples), BF16)
    return pl.pallas_call(
        pick_kernel,
        in_specs=[SMEM, VMEM, VMEM],
        out_specs=[VMEM] * 5,
        out_shape=[jax.ShapeDtypeStruct((ROWS, channels), BF16), slab, slab, rows, rows],
        compiler_params=pltpu.CompilerParams(vmem_limit_bytes=8 * MIB),
        name="picked_rows",
    )(place, small, traces)


def source_rows(place, pick, rows_high, rows_low, got_a, got_b, small):
    blocks = rows_high.shape[1] // LANES + 2 * EDGE
    return pl.pallas_call(
        source_kernel,
        in_specs=[SMEM] + [VMEM] * 6,
        out_specs=VMEM,
        out_shape=jax.ShapeDtypeStruct((blocks * MAX_OWN, LANES), BF16),
        compiler_params=pltpu.CompilerParams(vmem_limit_bytes=8 * MIB),
        name="source_rows",
    )(place, pick, rows_high, rows_low, got_a, got_b, small)


def normed_rows(place, small, high, low, got_a, got_b, owners, paired):
    channels, samples = high.shape
    return pl.pallas_call(
        functools.partial(normed_kernel, owners=owners, paired=paired),
        in_specs=[SMEM] + [VMEM] * 5,
        out_specs=[VMEM] * 2,
        out_shape=[
            jax.ShapeDtypeStruct((channels * samples // LANES, LANES), F32),
            jax.ShapeDtypeStruct((1, small.shape[1] - 3 * LANES), jnp.int32),
        ],
        compiler_params=pltpu.CompilerParams(vmem_limit_bytes=24 * MIB),
        cost_estimate=pl.CostEstimate(
            flops=2 * 5 * channels * samples * 3 * LANES,
            bytes_accessed=16 * channels * samples,
            transcendentals=0,
        ),
        name="normed_rows",
    )(place, high, low, got_a, got_b, small)


def shifted_rows(normed, channels):
    samples = normed.shape[0] // channels * LANES
    depth = -(-(samples + LANES) // TILE) * TILE
    return pl.pallas_call(
        functools.partial(shifted_kernel, channels=channels),
        in_specs=[VMEM],
        out_specs=VMEM,
        out_shape=jax.ShapeDtypeStruct((channels * LAG_WIDTH, depth), BF16),
        compiler_params=pltpu.CompilerParams(vmem_limit_bytes=4 * MIB),
        cost_estimate=pl.CostEstimate(
            flops=4 * channels * LAG_WIDTH * depth,
            bytes_accessed=2 * channels * LAG_WIDTH * depth,
            transcendentals=0,
        ),
        name="shifted_rows",
    )(normed)


def correlate(place, parts, shifted, sources, channels, samples):
    blocks = samples // LANES + 2 * EDGE
    rows = sum(part.shape[0] for part in parts)
    spare = -blocks % 8
    scale = 1.0 / math.sqrt(samples)
    boxes = pl.pallas_call(
        functools.partial(
            correlate_kernel,
            sources=sources,
            channels=channels,
            samples=samples,
            pieces=len(parts),
            scale=scale,
        ),
        grid=(channels // (UNITS * GROUP),),
        in_specs=[SMEM] + [VMEM] * len(parts) + [VMEM],
        out_specs=pl.BlockSpec(memory_space=pl.ANY),
        out_shape=jax.ShapeDtypeStruct(
            (sources, channels // GROUP, LAG_BLOCKS, GROUP, LANES), F32
        ),
        scratch_shapes=[
            pltpu.VMEM((rows + spare * MAX_OWN, LANES), F32),
            pltpu.VMEM(((blocks + 1 + spare) * (sources + 8), LANES), F32),
            pltpu.VMEM((LAG_BLOCKS * PIECES * sources, shifted.shape[1]), BF16),
            pltpu.VMEM((sources * (UNITS + 1) * (LAG_BLOCKS + 1) * GROUP, LANES), F32),
            pltpu.SemaphoreType.DMA((2 + UNITS * LAG_BLOCKS // 2,)),
        ],
        compiler_params=pltpu.CompilerParams(vmem_limit_bytes=24 * MIB),
        name="correlate",
    )(place, *parts, shifted)
    return boxes.transpose(0, 1, 3, 2, 4).reshape(sources, channels, 2 * LAG_HALF)


def body(traces, fir_taps, source_index):
    channels, samples = traces.shape
    taps = fir_taps.shape[0]
    slabs = lax.axis_size("tm")
    owners = lax.axis_size("chan")
    slab = lax.axis_index("tm")
    in_pairs = slabs % 2 == 0
    parity = slab % 2 if in_pairs else 0 * slab
    place = jnp.stack([slab, jnp.full_like(slab, slabs), parity, lax.axis_index("chan")])
    place = place.astype(jnp.int32)
    lead = LANES - (taps - 1) // 2
    total = 3 * LANES + source_index.shape[0]
    small = jnp.pad(fir_taps[None], ((0, 0), (lead, total - lead - taps)))
    small = small + jnp.pad(source_index[None].astype(F32), ((0, 0), (3 * LANES, 0)))

    left, right = traces[:, : SIDE * LANES], traces[:, samples - SIDE * LANES :]
    if in_pairs:
        edge_a, edge_b = jnp.where(parity == 0, right, left), jnp.where(parity == 0, left, right)
        got_b = lax.ppermute(edge_b, "tm", [(i, (i + 1 if i % 2 else i - 1) % slabs) for i in range(slabs)])
        got_a = lax.ppermute(edge_a, "tm", [(i, i ^ 1) for i in range(slabs)])
    else:
        got_b = lax.ppermute(right, "tm", [(i, i + 1) for i in range(slabs - 1)])
        got_a = lax.ppermute(left, "tm", [(i + 1, i) for i in range(slabs - 1)])
    pick, high, low, *rows = picked_rows(place, small, traces)
    own = source_rows(place, pick, *rows, got_a, got_b, small)
    paired = owners in (4, 8)
    normed, start = normed_rows(place, small, high, low, got_a, got_b, owners, paired)
    if paired:

        def swap(value, distance):
            return lax.ppermute(value, "chan", [(i, i ^ distance) for i in range(owners)])

        early = [swap(own, distance) for distance in EARLY]
        column = [swap(own, distance) for distance in range(2, owners, 2)]
        held = lax.optimization_barrier((*column, *early, normed))
        column, early, normed = list(held[: len(column)]), list(held[len(column) : -1]), held[-1]
        column = [own] + column
        late = jnp.concatenate(column[len(EARLY) :], axis=0)
        parts = column[: len(EARLY)] + [late] + early + [swap(late, 1)]
    else:
        parts = [lax.all_gather(own, "chan", axis=0, tiled=True)]
    shifted = shifted_rows(normed, channels)
    return correlate(start, parts, shifted, source_index.shape[0], channels, samples)[None]


def solution(mesh):
    placed = (P("chan", "tm"), P(), P())
    return jax.shard_map(
        body, mesh=mesh, in_specs=placed, out_specs=P("tm", None, "chan", None), check_vma=False
    )
```
